32 devices in a mesh: dp: 8 (over y, x, core), mp: 4 (over z).
Axes of the slice: x: 2, y: 2, z: 4, core: 2. Of those that a mesh axis runs over, the one named last changes fastest.
Arguments:
- tokens: bfloat16 [8192, 2048], P('dp'), may hold values from -6 to 6
- cotangent: bfloat16 [8192, 2048], P('dp'), may hold values from -6 to 6
- lengths: int32 [8], P('dp'), may hold values from 50 to 1024, as said below
- qkv_weight: float32 [2048, 3, 2048], P('dp', None, 'mp'), may hold values from -0.125 to 0.125
- out_weight: float32 [2048, 2048], P('mp', 'dp'), may hold values from -3 to 3
- gate_up_weight: float32 [2048, 2, 8192], P('dp', None, 'mp'), may hold values from -0.125 to 0.125
- down_weight: float32 [8192, 2048], P('mp', 'dp'), may hold values from -0.0625 to 0.0625
- norm_gains: float32 [2, 2048], P(None, 'dp'), may hold values from 0.25 to 1.75
- qkv_first: float32 [2048, 3, 2048], P('dp', None, 'mp')
- out_first: float32 [2048, 2048], P('mp', 'dp')
- gate_up_first: float32 [2048, 2, 8192], P('dp', None, 'mp')
- down_first: float32 [8192, 2048], P('mp', 'dp')
- gains_first: float32 [2, 2048], P(None, 'dp')
- qkv_second: float32 [2048, 3, 2048], P('dp', None, 'mp'), may hold values from 2048 to 8192
- out_second: float32 [2048, 2048], P('mp', 'dp'), may hold values from 8 to 32
- gate_up_second: float32 [2048, 2, 8192], P('dp', None, 'mp'), may hold values from 2048 to 8192
- down_second: float32 [8192, 2048], P('mp', 'dp'), may hold values from 2048 to 8192
- gains_second: float32 [2, 2048], P(None, 'dp'), may hold values from 8192 to 32768
Outputs:
- block_out: bfloat16 [8192, 2048], P(('dp', 'mp'))
- tokens_grad: float32 [8192, 2048], P(('dp', 'mp'))
- qkv_new: float32 [2048, 3, 2048], P('dp', None, 'mp')
- out_new: float32 [2048, 2048], P('mp', 'dp')
- gate_up_new: float32 [2048, 2, 8192], P('dp', None, 'mp')
- down_new: float32 [8192, 2048], P('mp', 'dp')
- gains_new: float32 [2, 2048], P(None, 'dp')
- qkv_first_new: float32 [2048, 3, 2048], P('dp', None, 'mp')
- out_first_new: float32 [2048, 2048], P('mp', 'dp')
- gate_up_first_new: float32 [2048, 2, 8192], P('dp', None, 'mp')
- down_first_new: float32 [8192, 2048], P('mp', 'dp')
- gains_first_new: float32 [2, 2048], P(None, 'dp')
- qkv_second_new: float32 [2048, 3, 2048], P('dp', None, 'mp')
- out_second_new: float32 [2048, 2048], P('mp', 'dp')
- gate_up_second_new: float32 [2048, 2, 8192], P('dp', None, 'mp')
- down_second_new: float32 [8192, 2048], P('mp', 'dp')
- gains_second_new: float32 [2, 2048], P(None, 'dp')
The draws below stay inside these ranges and needn't reach their ends.
Inputs may be any that keep to these rules, and one draw needn't show every extreme that they name: `lengths`: one sequence in every draw has all 1024 tokens valid.
All inputs are finite; a program needn't handle non-finite values.
Results may differ from the reference program's by a relative error of at most 0.014.
The reference program's roundings to bfloat16 on the way count: a program that leaves them out, or rounds other values in their place, can miss the bound.
Values may be sent and summed in bfloat16 or wider, within the bound.
No kernel may reach another device: no remote copies, remote signals or barrier semaphores. Data moves between devices by JAX's collectives and lax.ppermute only.
A program may use at most 384 MiB of HBM per device.

```python
import math
import jax
import jax.numpy as jnp
from jax import lax

D = 2048
H = 16
HD = 128
FF = 8192
SEQ = 1024
MIN_LEN = 50
STEP = 10
SEQS = 8
TOKENS = 8192


def moment_first(key, shape, scale):
    return scale * jax.random.normal(key, shape, jnp.float32)


def moment_second(key, shape, variance):
    unit_draw = jax.random.uniform(key, shape, jnp.float32)
    return variance * jnp.exp(unit_draw * math.log(4.0))


def draw_lengths(key, part):
    key = jax.random.fold_in(key, 3)
    left_key, right_key = jax.random.split(key)
    lengths_drawn = jax.random.randint(left_key, (SEQS,), MIN_LEN, SEQ + 1)
    longest = jax.random.randint(right_key, (), 0, SEQS)
    return jnp.where(jnp.arange(SEQS) == longest, SEQ, lengths_drawn).astype(jnp.int32)


def draw_qkv_first(key, part):
    key = jax.random.fold_in(key, 11)
    return moment_first(key, (D, 3, H * HD), 0.5 * math.sqrt(TOKENS))


def draw_out_first(key, part):
    key = jax.random.fold_in(key, 12)
    return moment_first(key, (H * HD, D), math.sqrt(TOKENS / SEQ))


def draw_gate_up_first(key, part):
    key = jax.random.fold_in(key, 13)
    return moment_first(key, (D, 2, FF), 0.5 * math.sqrt(TOKENS))


def draw_down_first(key, part):
    key = jax.random.fold_in(key, 14)
    return moment_first(key, (FF, D), 0.5 * math.sqrt(TOKENS))


def draw_gains_first(key, part):
    key = jax.random.fold_in(key, 15)
    return moment_first(key, (2, D), math.sqrt(TOKENS))


def draw_qkv_second(key, part):
    key = jax.random.fold_in(key, 21)
    return moment_second(key, (D, 3, H * HD), 0.25 * TOKENS)


def draw_out_second(key, part):
    key = jax.random.fold_in(key, 22)
    return moment_second(key, (H * HD, D), TOKENS / SEQ)


def draw_gate_up_second(key, part):
    key = jax.random.fold_in(key, 23)
    return moment_second(key, (D, 2, FF), 0.25 * TOKENS)


def draw_down_second(key, part):
    key = jax.random.fold_in(key, 24)
    return moment_second(key, (FF, D), 0.25 * TOKENS)


def draw_gains_second(key, part):
    key = jax.random.fold_in(key, 25)
    return moment_second(key, (2, D), 1.0 * TOKENS)


def block_scale(own_key, dims, pieces, smallest, largest):
    level, own = 1.0, jax.random.fold_in(own_key, 6)
    for dim, shards_of in pieces:
        draws = jnp.exp(jax.random.uniform(jax.random.fold_in(own, dim), (shards_of,), jnp.float32, smallest / len(pieces), largest / len(pieces)))
        level = level * jnp.repeat(draws, dims[dim] // shards_of).reshape([-1 if axis == dim else 1 for axis in range(len(dims))])
    return level


def normal_values(rng, shape, scale, most, cuts=(), kind=jnp.bfloat16):
    array = jax.random.normal(rng, shape, jnp.float32) * scale
    if len(cuts) > 0:
        array = block_scale(rng, shape, cuts, -0.22, 0.18) * array
    return jnp.clip(array, min=-most, max=most).astype(kind)


def setup_inputs(seed: int = 0) -> dict:
    keys = jax.random.split(jax.random.key(seed), 19)
    tokens = normal_values(keys[0], (TOKENS, D), 1.0, 6.0, ((0, 8),))
    cotangent = normal_values(keys[1], (TOKENS, D), 1.0, 6.0, ((0, 8),))
    lengths = draw_lengths(jax.random.fold_in(keys[18], 71), 0)
    qkv_weight = normal_values(keys[3], (D, 3, H * HD), D ** -0.5, 0.125, ((0, 8), (2, 4)), jnp.float32)
    out_weight = normal_values(keys[4], (H * HD, D), (max(1, 2 * H * HD // SEQ)) ** -0.5, 3.0, ((0, 4), (1, 8)), jnp.float32)
    gate_up_weight = normal_values(keys[5], (D, 2, FF), D ** -0.5, 0.125, ((0, 8), (2, 4)), jnp.float32)
    down_weight = normal_values(keys[6], (FF, D), FF ** -0.5, 0.0625, ((0, 4), (1, 8)), jnp.float32)
    norm_gains = jnp.clip(1.0 + 0.15 * jax.random.normal(keys[7], (2, D), jnp.float32), 0.25, 1.75)
    qkv_first = draw_qkv_first(jax.random.fold_in(keys[18], 71), 0)
    out_first = draw_out_first(jax.random.fold_in(keys[18], 71), 0)
    gate_up_first = draw_gate_up_first(jax.random.fold_in(keys[18], 71), 0)
    down_first = draw_down_first(jax.random.fold_in(keys[18], 71), 0)
    gains_first = draw_gains_first(jax.random.fold_in(keys[18], 71), 0)
    qkv_second = draw_qkv_second(jax.random.fold_in(keys[18], 71), 0)
    out_second = draw_out_second(jax.random.fold_in(keys[18], 71), 0)
    gate_up_second = draw_gate_up_second(jax.random.fold_in(keys[18], 71), 0)
    down_second = draw_down_second(jax.random.fold_in(keys[18], 71), 0)
    gains_second = draw_gains_second(jax.random.fold_in(keys[18], 71), 0)
    return {"tokens": tokens, "cotangent": cotangent, "lengths": lengths, "qkv_weight": qkv_weight, "out_weight": out_weight, "gate_up_weight": gate_up_weight, "down_weight": down_weight, "norm_gains": norm_gains, "qkv_first": qkv_first, "out_first": out_first, "gate_up_first": gate_up_first, "down_first": down_first, "gains_first": gains_first, "qkv_second": qkv_second, "out_second": out_second, "gate_up_second": gate_up_second, "down_second": down_second, "gains_second": gains_second}


highest = lax.Precision.HIGHEST
norm_eps = 1e-05
adam_eps = 1e-08
beta_first = 0.5
beta_second = 0.5
weight_decay = 0.1

@jax.custom_vjp
def low(v):
    return lax.optimization_barrier(v.astype(jnp.bfloat16)).astype(jnp.float32)

@jax.custom_vjp
def low_back(v):
    return v

def low_keep(v):
    return (low(v), None)

def low_pass(kept, grad):
    return (grad,)

def back_keep(v):
    return (v, None)

def back_low(kept, grad):
    return (low(grad),)
low.defvjp(low_keep, low_pass)
low_back.defvjp(back_keep, back_low)

def step_rates():
    return (0.8 / math.sqrt(D), 0.8 / math.sqrt(max(1, 2 * H * HD // SEQ)), 0.8 / math.sqrt(D), 0.8 / math.sqrt(FF), 0.4)

def rope_tables():
    halfway = HD // 2
    inverse = jnp.exp(-math.log(10000.0) * jnp.arange(halfway, dtype=jnp.float32) * 2.0 / HD)
    angles = jnp.arange(SEQ, dtype=jnp.float32)[:, None] * inverse[None, :]
    return (jnp.cos(angles), jnp.sin(angles))

def rotate(vectors, cosine, sine_table):
    halfway = HD // 2
    front_half = vectors[..., :halfway]
    behind = vectors[..., halfway:]
    cos_wide = cosine[:, None, :]
    sin_wide = sine_table[:, None, :]
    return jnp.concatenate([front_half * cos_wide - behind * sin_wide, behind * cos_wide + front_half * sin_wide], axis=-1)

def rms_norm(values, gain):
    inverse = lax.rsqrt(lax.optimization_barrier(jnp.mean(values * values, axis=-1, keepdims=True)) + norm_eps)
    return values * inverse * gain

def forward(tokens32, lengths, qkv_weight, out_weight, gate_up_weight, down_weight, norm_gains):
    groups = tokens32.shape[0]
    gain_low = low(norm_gains)
    cosine, sine_table = rope_tables()
    normed = low(rms_norm(tokens32, gain_low[0]))
    project = jnp.einsum('gsd,dkf->gskf', normed, low(qkv_weight), precision=highest)
    project = low_back(project).reshape(groups, SEQ, 3, H, HD)
    queries = low(rotate(project[:, :, 0], cosine, sine_table))
    keys_rot = low(rotate(project[:, :, 1], cosine, sine_table))
    values = low(project[:, :, 2])
    scores = jnp.einsum('gshe,gthe->ghst', queries, keys_rot, precision=highest) / math.sqrt(HD) - math.log(SEQ)
    scores = low_back(scores)
    row_ids = jnp.arange(SEQ, dtype=jnp.int32)[:, None]
    col_ids = jnp.arange(SEQ, dtype=jnp.int32)[None, :]
    allowed = (col_ids <= row_ids)[None, None] & (col_ids[None, None] < lengths[:, None, None, None])
    attn_weights = low(jax.nn.sigmoid(scores) * allowed.astype(jnp.float32))
    mixed_heads = jnp.einsum('ghst,gthe->gshe', attn_weights, values, precision=highest).reshape(groups, SEQ, H * HD)
    mixed_heads = low(low_back(mixed_heads))
    attended = low_back(jnp.einsum('gsa,ad->gsd', mixed_heads, low(out_weight), precision=highest))
    middle = tokens32 + attended
    normed_two = low(rms_norm(middle, gain_low[1]))
    gate_up = low_back(jnp.einsum('gsd,dkf->gskf', normed_two, low(gate_up_weight), precision=highest))
    hidden = low(jax.nn.silu(gate_up[:, :, 0]) * gate_up[:, :, 1])
    feed_out = low_back(jnp.einsum('gsf,fd->gsd', hidden, low(down_weight), precision=highest))
    return middle + feed_out

def adamw(weight, moment_one, moment_two, gradient, step_rate):
    first_new = beta_first * moment_one + (1.0 - beta_first) * gradient
    second_new = beta_second * moment_two + (1.0 - beta_second) * gradient * gradient
    first_hat = first_new / (1.0 - beta_first ** STEP)
    second_hat = second_new / (1.0 - beta_second ** STEP)
    weight_new = weight - step_rate * (first_hat / (jnp.sqrt(second_hat) + adam_eps) + weight_decay * weight)
    return (weight_new, first_new, second_new)

def reference(tokens, cotangent, lengths, qkv_weight, out_weight, gate_up_weight, down_weight, norm_gains, qkv_first, out_first, gate_up_first, down_first, gains_first, qkv_second, out_second, gate_up_second, down_second, gains_second):
    group_size = min(SEQS, max(1, 2048 // SEQ))
    group_count = SEQS // group_size
    inputs = tokens.astype(jnp.float32).reshape(group_count, group_size, SEQ, D)
    back_rows = cotangent.astype(jnp.float32).reshape(group_count, group_size, SEQ, D)
    span_rows = lengths.reshape(group_count, group_size)
    params = (qkv_weight, out_weight, gate_up_weight, down_weight, norm_gains)

    def one_group(totals, group_item):
        block_in, block_back, block_len = group_item

        def run_block(block, *weights):
            return forward(block, block_len, *weights)
        result_rows, pullback = jax.vjp(run_block, block_in, *params)
        gradients = pullback(block_back)
        totals = tuple((running + gradient for running, gradient in zip(totals, gradients[1:])))
        return (totals, (result_rows.astype(jnp.bfloat16), gradients[0]))
    start_sums = tuple((jnp.zeros_like(parameter) for parameter in params))
    totals, (outputs, in_grads) = lax.scan(one_group, start_sums, (inputs, back_rows, span_rows))
    rates = step_rates()
    qkv_all = adamw(qkv_weight, qkv_first, qkv_second, totals[0], rates[0])
    out_all = adamw(out_weight, out_first, out_second, totals[1], rates[1])
    gate_up_all = adamw(gate_up_weight, gate_up_first, gate_up_second, totals[2], rates[2])
    down_all = adamw(down_weight, down_first, down_second, totals[3], rates[3])
    gains_all = adamw(norm_gains, gains_first, gains_second, totals[4], rates[4])
    return (outputs.reshape(TOKENS, D), in_grads.reshape(TOKENS, D), qkv_all[0], out_all[0], gate_up_all[0], down_all[0], gains_all[0], qkv_all[1], out_all[1], gate_up_all[1], down_all[1], gains_all[1], qkv_all[2], out_all[2], gate_up_all[2], down_all[2], gains_all[2])
```

```python
import math

import jax
import jax.numpy as jnp
from jax import lax
from jax.sharding import PartitionSpec as P

D = 2048
H = 16
HD = 128
FF = 8192
SEQ = 1024
STEP = 10


norm_eps = 1e-05
adam_eps = 1e-08
beta_first = 0.5
beta_second = 0.5
weight_decay = 0.1


def step_rates():
    return (
        0.8 / math.sqrt(D),
        0.8 / math.sqrt(max(1, 2 * H * HD // SEQ)),
        0.8 / math.sqrt(D),
        0.8 / math.sqrt(FF),
        0.4,
    )


def rope_tables():
    halfway = HD // 2
    inverse = jnp.exp(-math.log(10000.0) * jnp.arange(halfway, dtype=jnp.float32) * 2.0 / HD)
    angles = jnp.arange(SEQ, dtype=jnp.float32)[:, None] * inverse[None, :]
    return (jnp.cos(angles), jnp.sin(angles))


def rotate(vectors, cosine, sine_table):
    halfway = HD // 2
    front_half = vectors[..., :halfway]
    behind = vectors[..., halfway:]
    return jnp.concatenate(
        [front_half * cosine - behind * sine_table, behind * cosine + front_half * sine_table],
        axis=-1,
    )


def norm_forward(values, gain):
    inverse = lax.rsqrt(jnp.mean(values * values, axis=-1, keepdims=True) + norm_eps)
    return (values * inverse * gain, inverse)


def norm_backward(values, inverse, gain, upstream):
    scaled = upstream * gain
    gain_grad = jnp.sum(upstream * values * inverse, axis=0)
    values_grad = inverse * scaled - values * inverse * inverse * inverse * jnp.mean(
        scaled * values, axis=-1, keepdims=True
    )
    return (values_grad, gain_grad)


def block_mask(begin_row, end_row, valid_len):
    row_ids = begin_row + jnp.arange(end_row - begin_row, dtype=jnp.int32)[:, None]
    col_ids = jnp.arange(end_row, dtype=jnp.int32)[None, :]
    return ((col_ids <= row_ids) & (col_ids < valid_len)).astype(jnp.float32)


def block_scores(query_block, keys_rot, end_row):
    raw = jnp.einsum(
        "hqe,hke->hqk", query_block, keys_rot[:, :end_row], preferred_element_type=jnp.float32
    )
    return raw / math.sqrt(HD) - math.log(SEQ)


def attend_forward(queries, keys_rot, values, valid_len):
    block_rows = min(512, SEQ)
    pieces = []
    for begin_row in range(0, SEQ, block_rows):
        end_row = begin_row + block_rows
        scores = block_scores(queries[:, begin_row:end_row], keys_rot, end_row)
        weights_p = jax.nn.sigmoid(scores) * block_mask(begin_row, end_row, valid_len)
        pieces.append(
            jnp.einsum(
                "hqk,hke->hqe",
                weights_p.astype(jnp.bfloat16),
                values[:, :end_row],
                preferred_element_type=jnp.float32,
            )
        )
    return jnp.concatenate(pieces, axis=1)


def attend_backward(queries, keys_rot, values, mixed_back, valid_len):
    block_rows = min(512, SEQ)
    query_parts = []
    key_back = jnp.zeros(keys_rot.shape, jnp.float32)
    value_back = jnp.zeros(values.shape, jnp.float32)
    for begin_row in range(0, SEQ, block_rows):
        end_row = begin_row + block_rows
        query_block = queries[:, begin_row:end_row]
        back_block = mixed_back[:, begin_row:end_row]
        scores = block_scores(query_block, keys_rot, end_row)
        mask_block = block_mask(begin_row, end_row, valid_len)
        sigmoid_val = jax.nn.sigmoid(scores)
        weights_p = (sigmoid_val * mask_block).astype(jnp.bfloat16)
        value_back = value_back.at[:, :end_row].add(
            jnp.einsum("hqk,hqe->hke", weights_p, back_block, preferred_element_type=jnp.float32)
        )
        weight_back = jnp.einsum(
            "hqe,hke->hqk", back_block, values[:, :end_row], preferred_element_type=jnp.float32
        )
        score_back = (weight_back * mask_block * sigmoid_val * (1.0 - sigmoid_val)).astype(
            jnp.bfloat16
        )
        query_parts.append(
            jnp.einsum(
                "hqk,hke->hqe",
                score_back,
                keys_rot[:, :end_row],
                preferred_element_type=jnp.float32,
            )
            / math.sqrt(HD)
        )
        key_back = key_back.at[:, :end_row].add(
            jnp.einsum("hqk,hqe->hke", score_back, query_block, preferred_element_type=jnp.float32)
            / math.sqrt(HD)
        )
    return (jnp.concatenate(query_parts, axis=1), key_back, value_back)


def split_heads(block, seq_count, local_heads):
    return block.reshape(seq_count, SEQ, local_heads, HD).transpose(0, 2, 1, 3)


def merge_heads(block, seq_count, local_heads):
    return block.transpose(0, 2, 1, 3).reshape(seq_count * SEQ, local_heads * HD)


def adamw(weight, moment_one, moment_two, gradient, step_rate):
    first_new = beta_first * moment_one + (1.0 - beta_first) * gradient
    second_new = beta_second * moment_two + (1.0 - beta_second) * gradient * gradient
    first_hat = first_new / (1.0 - beta_first**STEP)
    second_hat = second_new / (1.0 - beta_second**STEP)
    weight_new = weight - step_rate * (
        first_hat / (jnp.sqrt(second_hat) + adam_eps) + weight_decay * weight
    )
    return (weight_new, first_new, second_new)


def shift_all(block, take=None):
    size = lax.axis_size("mp")
    got = [block if take is None else take(0)]
    for k in range(1, size):
        send = block if take is None else take(k)
        got.append(lax.ppermute(send, "mp", [(j, (j + k) % size) for j in range(size)]))
    return got


def exchange_rows(full):
    size = lax.axis_size("mp")
    me = lax.axis_index("mp")
    rows = full.shape[0] // size

    def take(k):
        return lax.dynamic_slice_in_dim(full, lax.rem(me + k, size) * rows, rows, 0)

    return shift_all(None, take)


def sum_f32(parts):
    total = parts[0].astype(jnp.float32)
    for part in parts[1:]:
        total = total + part.astype(jnp.float32)
    return total


def local(
    tokens,
    cotangent,
    lengths,
    qkv_weight,
    out_weight,
    gate_up_weight,
    down_weight,
    norm_gains,
    qkv_first,
    out_first,
    gate_up_first,
    down_first,
    gains_first,
    qkv_second,
    out_second,
    gate_up_second,
    down_second,
    gains_second,
):
    bf16 = jnp.bfloat16
    f32 = jnp.float32
    size = lax.axis_size("mp")
    me = lax.axis_index("mp")
    qkv_full = lax.all_gather(qkv_weight.astype(bf16), "dp", axis=0, tiled=True)
    gain_low = lax.all_gather(norm_gains.astype(bf16), "dp", axis=1, tiled=True)
    out_parts = shift_all(out_weight.astype(bf16))
    out_rows = jnp.zeros((size,) + out_weight.shape, bf16)
    for k in range(size):
        out_rows = lax.dynamic_update_index_in_dim(
            out_rows, out_parts[k], lax.rem(me - k + size, size), 0
        )
    out_full = lax.all_gather(out_rows.reshape(-1, out_weight.shape[1]), "dp", axis=1, tiled=True)
    gate_up_full = lax.all_gather(gate_up_weight.astype(bf16), "dp", axis=0, tiled=True)
    down_full = lax.all_gather(down_weight.astype(bf16), "dp", axis=1, tiled=True)
    seq_count = lengths.shape[0]
    local_heads = qkv_full.shape[2] // HD
    head_cols = qkv_full.shape[2]
    cosine, sine_table = rope_tables()
    row_count = tokens.shape[0] // size
    row_start = me * row_count

    def own_rows(block):
        return lax.dynamic_slice_in_dim(block, row_start, row_count, 0)

    tokens32 = tokens.astype(f32)
    gain_one = gain_low[0].astype(f32)
    gain_two = gain_low[1].astype(f32)
    normed, scale_one = norm_forward(tokens32, gain_one)
    normed_bf = normed.astype(bf16)
    project = jnp.einsum("nd,dkf->nkf", normed_bf, qkv_full, preferred_element_type=f32)
    queries = rotate(split_heads(project[:, 0], seq_count, local_heads), cosine, sine_table).astype(
        bf16
    )
    keys_rot = rotate(
        split_heads(project[:, 1], seq_count, local_heads), cosine, sine_table
    ).astype(bf16)
    values = split_heads(project[:, 2], seq_count, local_heads).astype(bf16)
    mixed = lax.map(
        lambda seq_item: attend_forward(*seq_item), (queries, keys_rot, values, lengths)
    )
    mixed_bf = merge_heads(mixed, seq_count, local_heads).astype(bf16)
    mixed_parts = shift_all(mixed_bf)
    attended = None
    mixed_own = jnp.zeros((row_count, size, head_cols), bf16)
    for k in range(size):
        owner = lax.rem(me - k + size, size)
        rows_of = lax.dynamic_slice_in_dim(out_full, owner * head_cols, head_cols, 0)
        term = jnp.dot(mixed_parts[k], rows_of, preferred_element_type=f32)
        attended = term if attended is None else attended + term
        mixed_own = lax.dynamic_update_slice_in_dim(
            mixed_own, own_rows(mixed_parts[k])[:, None], owner, 1
        )
    mixed_own = mixed_own.reshape(row_count, size * head_cols)
    middle = tokens32 + attended
    normed_two, scale_two = norm_forward(middle, gain_two)
    normed_two_bf = normed_two.astype(bf16)
    middle_own = own_rows(middle)
    scale_own = own_rows(scale_two)
    gate_up = jnp.einsum("nd,dkf->nkf", normed_two_bf, gate_up_full, preferred_element_type=f32)
    gate_val = gate_up[:, 0]
    up_val = gate_up[:, 1]
    gate_sig = jax.nn.sigmoid(gate_val)
    silu_val = gate_val * gate_sig
    hidden_bf = (silu_val * up_val).astype(bf16)
    hidden_back = jnp.einsum("nd,fd->nf", cotangent, down_full, preferred_element_type=f32)
    gate_grad = hidden_back * up_val * gate_sig * (1.0 + gate_val * (1.0 - gate_sig))
    up_grad = hidden_back * silu_val
    gate_up_back = jnp.stack([gate_grad, up_grad], axis=1).astype(bf16)
    two_back_part = jnp.einsum(
        "nkf,dkf->nd", gate_up_back, gate_up_full, preferred_element_type=f32
    ).astype(bf16)
    two_back_parts = exchange_rows(two_back_part)
    feed_part = jnp.dot(hidden_bf, down_full, preferred_element_type=f32).astype(bf16)
    normed_two_back = sum_f32(two_back_parts)
    middle_back, gain_two_grad = norm_backward(middle_own, scale_own, gain_two, normed_two_back)
    middle_back = middle_back + own_rows(cotangent).astype(f32)
    middle_low = middle_back.astype(bf16)
    mixed_back = jnp.einsum("nd,ad->na", middle_low, out_full, preferred_element_type=f32).astype(
        bf16
    )

    def heads_of(k):
        return lax.dynamic_slice_in_dim(mixed_back, lax.rem(me + k, size) * head_cols, head_cols, 1)

    back_parts = shift_all(None, heads_of)
    mixed_heads = jnp.zeros((size, row_count, head_cols), bf16)
    for k in range(size):
        mixed_heads = lax.dynamic_update_index_in_dim(
            mixed_heads, back_parts[k], lax.rem(me - k + size, size), 0
        )
    feed_part, mixed_heads = lax.optimization_barrier((feed_part, mixed_heads))
    feed_parts = exchange_rows(feed_part)
    mixed_back = split_heads(mixed_heads.reshape(-1, head_cols), seq_count, local_heads)

    down_grad = jnp.einsum("nf,nd->fd", hidden_bf, cotangent, preferred_element_type=f32)
    gate_up_grad = jnp.einsum(
        "nd,nkf->dkf", normed_two_bf, gate_up_back, preferred_element_type=f32
    )
    gate_up_red = lax.psum_scatter(gate_up_grad.astype(bf16), "dp", scatter_dimension=0, tiled=True)
    down_red = lax.psum_scatter(down_grad.astype(bf16), "dp", scatter_dimension=1, tiled=True)
    out_grad = jnp.einsum("na,nd->ad", mixed_own, middle_low, preferred_element_type=f32)
    out_red = lax.psum_scatter(out_grad.astype(bf16), "dp", scatter_dimension=1, tiled=True)
    out_sum = sum_f32(exchange_rows(out_red))

    query_back, key_back, value_back = lax.map(
        lambda seq_item: attend_backward(*seq_item),
        (queries, keys_rot, values, mixed_back, lengths),
    )
    query_back = rotate(query_back, cosine, -sine_table)
    key_back = rotate(key_back, cosine, -sine_table)
    project_back = jnp.stack(
        [
            merge_heads(query_back, seq_count, local_heads),
            merge_heads(key_back, seq_count, local_heads),
            merge_heads(value_back, seq_count, local_heads),
        ],
        axis=1,
    ).astype(bf16)
    one_back_part = jnp.einsum(
        "nkf,dkf->nd", project_back, qkv_full, preferred_element_type=f32
    )
    one_back_low = one_back_part.astype(bf16)
    one_back_parts = exchange_rows(one_back_low)
    gain_one_grad = jnp.sum(one_back_low.astype(f32) * tokens32 * scale_one, axis=0)
    qkv_grad = jnp.einsum("nd,nkf->dkf", normed_bf, project_back, preferred_element_type=f32)
    qkv_red = lax.psum_scatter(qkv_grad.astype(bf16), "dp", scatter_dimension=0, tiled=True)
    gains_part = lax.psum_scatter(
        jnp.stack([gain_one_grad, gain_two_grad]), "dp", scatter_dimension=1, tiled=True
    )
    gains_red = sum_f32(shift_all(gains_part))
    normed_back = sum_f32(one_back_parts)
    tokens_part, _ = norm_backward(own_rows(tokens32), own_rows(scale_one), gain_one, normed_back)
    tokens_grad = tokens_part + middle_back
    block_out = (middle_own + sum_f32(feed_parts)).astype(bf16)
    rates = step_rates()
    qkv_all = adamw(qkv_weight, qkv_first, qkv_second, qkv_red.astype(f32), rates[0])
    out_all = adamw(out_weight, out_first, out_second, out_sum, rates[1])
    gate_up_all = adamw(gate_up_weight, gate_up_first, gate_up_second, gate_up_red.astype(f32), rates[2])
    down_all = adamw(down_weight, down_first, down_second, down_red.astype(f32), rates[3])
    gains_all = adamw(norm_gains, gains_first, gains_second, gains_red, rates[4])
    states = (qkv_all, out_all, gate_up_all, down_all, gains_all)
    return (block_out, tokens_grad) + tuple(state[j] for j in range(3) for state in states)


def solution(mesh):
    in_specs = (
        P("dp", None),
        P("dp", None),
        P("dp"),
        P("dp", None, "mp"),
        P("mp", "dp"),
        P("dp", None, "mp"),
        P("mp", "dp"),
        P(None, "dp"),
        P("dp", None, "mp"),
        P("mp", "dp"),
        P("dp", None, "mp"),
        P("mp", "dp"),
        P(None, "dp"),
        P("dp", None, "mp"),
        P("mp", "dp"),
        P("dp", None, "mp"),
        P("mp", "dp"),
        P(None, "dp"),
    )
    out_specs = (
        P(("dp", "mp"), None),
        P(("dp", "mp"), None),
        P("dp", None, "mp"),
        P("mp", "dp"),
        P("dp", None, "mp"),
        P("mp", "dp"),
        P(None, "dp"),
        P("dp", None, "mp"),
        P("mp", "dp"),
        P("dp", None, "mp"),
        P("mp", "dp"),
        P(None, "dp"),
        P("dp", None, "mp"),
        P("mp", "dp"),
        P("dp", None, "mp"),
        P("mp", "dp"),
        P(None, "dp"),
    )
    return jax.shard_map(local, mesh=mesh, in_specs=in_specs, out_specs=out_specs, check_vma=False)
```

```python
import functools
import math

import jax
import jax.numpy as jnp
from jax import lax
from jax.experimental import pallas as pl
from jax.experimental.pallas import tpu as pltpu
from jax.sharding import PartitionSpec as P

D = 2048
H = 16
HD = 128
FF = 8192
SEQ = 1024
STEP = 10
VMEM = 56 << 20


norm_eps = 1e-05
adam_eps = 1e-08
beta_first = 0.5
beta_second = 0.5
weight_decay = 0.1


def step_rates():
    return (
        0.8 / math.sqrt(D),
        0.8 / math.sqrt(max(1, 2 * H * HD // SEQ)),
        0.8 / math.sqrt(D),
        0.8 / math.sqrt(FF),
        0.4,
    )


def rope_tables():
    halfway = HD // 2
    inverse = jnp.exp(-math.log(10000.0) * jnp.arange(halfway, dtype=jnp.float32) * 2.0 / HD)
    angles = jnp.arange(SEQ, dtype=jnp.float32)[:, None] * inverse[None, :]
    return (jnp.cos(angles), jnp.sin(angles))


def norm_forward(values, gain):
    inverse = lax.rsqrt(jnp.mean(values * values, axis=-1, keepdims=True) + norm_eps)
    return (values * inverse * gain, inverse)


def norm_backward(values, inverse, gain, upstream):
    scaled = upstream * gain
    gain_grad = jnp.sum(upstream * values * inverse, axis=0)
    values_grad = inverse * scaled - values * inverse * inverse * inverse * jnp.mean(
        scaled * values, axis=-1, keepdims=True
    )
    return (values_grad, gain_grad)


def adamw(weight, moment_one, moment_two, gradient, step_rate):
    first_new = beta_first * moment_one + (1.0 - beta_first) * gradient
    second_new = beta_second * moment_two + (1.0 - beta_second) * gradient * gradient
    first_hat = first_new / (1.0 - beta_first**STEP)
    second_hat = second_new / (1.0 - beta_second**STEP)
    weight_new = weight - step_rate * (
        first_hat / (jnp.sqrt(second_hat) + adam_eps) + weight_decay * weight
    )
    return (weight_new, first_new, second_new)


CORE, ALONG_X, ALONG_Y = 1, 2, 4
DIAGONAL = ALONG_X + ALONG_Y


def flip(block, bits, name="dp"):
    return lax.ppermute(block, name, [(j, j ^ bits) for j in range(lax.axis_size(name))])


def pick(block, place, width, axis):
    return lax.dynamic_slice_in_dim(block, place * width, width, axis)


def gather_near(shard):
    if lax.axis_size("dp") != 8:
        return [lax.all_gather(shard, "dp", axis=1, tiled=True)], None
    from_x = flip(shard, ALONG_X)
    from_y = flip(shard, ALONG_Y)
    from_core = flip(shard, CORE)
    upper = flip(from_y[:1], ALONG_X)
    lower = flip(from_x[1:], ALONG_Y)
    near = [shard, from_core, from_x, from_y, flip(from_x, CORE), flip(from_y, CORE)]
    return near, (upper, lower)


def gather_far(near, halves, after):
    if halves is None:
        return near, [0]
    me = lax.axis_index("dp")
    upper, lower = halves
    far = jnp.concatenate([tie(upper, after), tie(lower, after)], axis=0)
    bits = [0, CORE, ALONG_X, ALONG_Y, ALONG_X + CORE, ALONG_Y + CORE, DIAGONAL, DIAGONAL + CORE]
    return near + [far, flip(far, CORE)], [me ^ b for b in bits]


def core_columns(block, core):
    width = block.shape[1] // 8
    return jnp.concatenate([pick(block, 2 * q + core, width, 1) for q in range(4)], axis=1)


def reduce_dp(products, sharded, axis, after=()):
    f32, bf16 = jnp.float32, jnp.bfloat16
    if lax.axis_size("dp") != 8:
        full = [part.astype(bf16) for part in products(sharded)]
        done = [lax.psum_scatter(part, "dp", scatter_dimension=axis, tiled=True) for part in full]
        return [part.astype(f32) for part in done], full
    me = lax.axis_index("dp")
    core = lax.rem(me, 2)
    chip = lax.div(me, 2)
    other = [part.astype(bf16) for part in products(core_columns(sharded, 1 - core))]
    other = [flip(part, CORE) for part in other]
    own = products(core_columns(sharded, core))
    total = [(a + b.astype(f32)).astype(bf16) for a, b in zip(own, other)]
    width = total[0].shape[axis] // 4
    upper = flip(pick(total[0], chip ^ 3, width, axis), ALONG_X)
    lower = flip(pick(total[1], chip ^ 3, width, axis), ALONG_Y)
    if after:
        upper, lower = tie(upper, *after), tie(lower, *after)
    near_x = [pick(part, chip ^ 1, width, axis) for part in total]
    near_y = [pick(part, chip ^ 2, width, axis) for part in total]
    to_x = jnp.stack([near_x[0], (near_x[1].astype(f32) + lower.astype(f32)).astype(bf16)])
    to_y = jnp.stack([(near_y[0].astype(f32) + upper.astype(f32)).astype(bf16), near_y[1]])
    from_x = flip(to_x, ALONG_X)
    from_y = flip(to_y, ALONG_Y)
    mine = [pick(part, chip, width, axis).astype(f32) for part in total]
    return [mine[k] + from_x[k].astype(f32) + from_y[k].astype(f32) for k in range(2)], total


def shift_all(take):
    size = lax.axis_size("mp")
    got = [take(0)]
    for k in range(1, size):
        got.append(lax.ppermute(take(k), "mp", [(j, (j + k) % size) for j in range(size)]))
    return got


def gather_line(block):
    size = lax.axis_size("mp")
    me = lax.axis_index("mp")
    if size != 4:
        parts = shift_all(lambda k: block)
        return parts, [lax.rem(me - k + size, size) for k in range(size)]
    from_low = lax.ppermute(block, "mp", [(0, 1), (1, 2), (2, 3)])
    from_high = lax.ppermute(block, "mp", [(1, 0), (2, 1), (3, 2)])
    inward = jnp.where(me == 1, from_low, from_high)
    outward = jnp.where(me == 1, from_high, from_low)
    end = lax.ppermute(inward, "mp", [(2, 0), (1, 3)])
    middle = lax.ppermute(inward, "mp", [(2, 1), (1, 2)])
    edge = lax.ppermute(outward, "mp", [(1, 0), (2, 3)])
    low, high = lax.rem(me + 3, 4), lax.rem(me + 1, 4)
    end_owner = jnp.where(me == 0, 3, jnp.where(me == 3, 0, me))
    return [block, from_low, from_high, end, middle + edge], [
        me,
        low,
        high,
        end_owner,
        lax.rem(me + 2, 4),
    ]


def sum_flips(block, name):
    bits = 1
    while bits < lax.axis_size(name):
        block = block + flip(block, bits, name)
        bits *= 2
    return block


def rotate_wide(block, cosine, sine):
    heads = block.shape[1] // HD
    parts = []
    for h in range(heads):
        head = block[:, h * HD : (h + 1) * HD]
        parts.append(head * cosine + pltpu.roll(head, HD // 2, 1) * sine)
    return parts[0] if heads == 1 else jnp.concatenate(parts, axis=1)


def project_kernel(normed_ref, weight_ref, cosine_ref, sine_ref, out_ref):
    rows = normed_ref.shape[0]
    step = min(1024, rows)
    for begin in range(0, rows, step):
        block = jnp.dot(
            normed_ref[begin : begin + step], weight_ref[...], preferred_element_type=jnp.float32
        )

        @pl.when(pl.program_id(0) < 2)
        def _(block=block, begin=begin):
            out_ref[begin : begin + step] = rotate_wide(
                block, cosine_ref[begin : begin + step], sine_ref[begin : begin + step]
            ).astype(out_ref.dtype)

        @pl.when(pl.program_id(0) == 2)
        def _(block=block, begin=begin):
            out_ref[begin : begin + step] = block.astype(out_ref.dtype)


def project_heads(normed, weight, cosine, sine):
    rows, width = normed.shape
    cols = weight.shape[1] // 3
    return pl.pallas_call(
        project_kernel,
        grid=(3,),
        in_specs=[
            pl.BlockSpec((rows, width), lambda c: (0, 0)),
            pl.BlockSpec((width, cols), lambda c: (0, c)),
            pl.BlockSpec((rows, HD), lambda c: (0, 0)),
            pl.BlockSpec((rows, HD), lambda c: (0, 0)),
        ],
        out_specs=pl.BlockSpec((rows, cols), lambda c: (0, c)),
        out_shape=jax.ShapeDtypeStruct((rows, 3 * cols), jnp.bfloat16),
        compiler_params=pltpu.CompilerParams(vmem_limit_bytes=VMEM),
        cost_estimate=pl.CostEstimate(flops=1, bytes_accessed=1, transcendentals=0),
    )(normed, weight, cosine, sine)


def transposed_dot(a, b):
    return lax.dot_general(a, b, (((1,), (1,)), ((), ())), preferred_element_type=jnp.float32)


def lead_dot(a, b):
    return lax.dot_general(a, b, (((0,), (0,)), ((), ())), preferred_element_type=jnp.float32)


def causal_sigmoid(scores_raw, begin):
    rows, cols = scores_raw.shape
    grown = jnp.exp(math.log(SEQ) - scores_raw * (1.0 / math.sqrt(HD)))
    sigmoid_val = 1.0 / (1.0 + grown)
    row_ids = begin + lax.broadcasted_iota(jnp.int32, (rows, rows), 0)
    col_ids = begin + lax.broadcasted_iota(jnp.int32, (rows, rows), 1)
    last = jnp.where(col_ids <= row_ids, sigmoid_val[:, cols - rows :], 0.0)
    if cols == rows:
        return last
    return jnp.concatenate([sigmoid_val[:, : cols - rows], last], axis=1)


def keep_valid(block, valid_len):
    ids = lax.broadcasted_iota(jnp.int32, block.shape, 0)
    return jnp.where(ids < valid_len, block, jnp.zeros_like(block))


def attend_kernel(lengths_ref, query_ref, key_ref, value_ref, out_ref):
    valid_len = lengths_ref[pl.program_id(0)]
    keys = key_ref[...]
    values = keep_valid(value_ref[...], valid_len)
    step = min(256, SEQ)
    for begin in range(0, SEQ, step):
        end = begin + step
        weights = causal_sigmoid(transposed_dot(query_ref[begin:end], keys[:end]), begin)
        out_ref[begin:end] = jnp.dot(
            weights.astype(jnp.bfloat16), values[:end], preferred_element_type=jnp.float32
        ).astype(out_ref.dtype)


def attend(lengths, heads_all):
    rows, width = heads_all.shape
    heads = width // 3 // HD

    def spec(part):
        return pl.BlockSpec((SEQ, HD), lambda s, h, *_: (s, part * heads + h))

    return pl.pallas_call(
        attend_kernel,
        grid_spec=pltpu.PrefetchScalarGridSpec(
            num_scalar_prefetch=1,
            grid=(rows // SEQ, heads),
            in_specs=[spec(0), spec(1), spec(2)],
            out_specs=pl.BlockSpec((SEQ, HD), lambda s, h, *_: (s, h)),
        ),
        out_shape=jax.ShapeDtypeStruct((rows, width // 3), jnp.bfloat16),
        compiler_params=pltpu.CompilerParams(vmem_limit_bytes=VMEM),
        cost_estimate=pl.CostEstimate(flops=1, bytes_accessed=1, transcendentals=0),
    )(lengths, heads_all, heads_all, heads_all)


def attend_back_kernel(
    heads,
    lengths_ref,
    query_ref,
    key_ref,
    value_ref,
    back_ref,
    cosine_ref,
    sine_ref,
    out_ref,
    key_total,
    value_total,
):
    valid_len = lengths_ref[pl.program_id(0)]
    head = pl.program_id(1)
    keys = key_ref[...]
    keys_kept = keep_valid(keys, valid_len)
    values = value_ref[...]
    key_total[...] = jnp.zeros_like(key_total)
    value_total[...] = jnp.zeros_like(value_total)
    step = min(256, SEQ)

    def column(part):
        return pl.ds(pl.multiple_of(part * heads * HD + head * HD, HD), HD)

    for begin in range(0, SEQ, step):
        end = begin + step
        queries = query_ref[begin:end]
        back = back_ref[begin:end]
        weights = causal_sigmoid(transposed_dot(queries, keys[:end]), begin)
        value_total[:end] += lead_dot(weights.astype(jnp.bfloat16), back)
        weight_back = transposed_dot(back, values[:end])
        score_back = (weight_back * (weights * (1.0 - weights))).astype(jnp.bfloat16)
        query_back = jnp.dot(
            score_back, keys_kept[:end], preferred_element_type=jnp.float32
        ) * (1.0 / math.sqrt(HD))
        key_total[:end] += lead_dot(score_back, queries)
        out_ref[begin:end, column(0)] = rotate_wide(
            query_back, cosine_ref[begin:end], sine_ref[begin:end]
        ).astype(out_ref.dtype)
    key_back = keep_valid(key_total[...] * (1.0 / math.sqrt(HD)), valid_len)
    out_ref[:, column(1)] = rotate_wide(key_back, cosine_ref[...], sine_ref[...]).astype(
        out_ref.dtype
    )
    out_ref[:, column(2)] = keep_valid(value_total[...], valid_len).astype(out_ref.dtype)


def attend_back(lengths, heads_all, mixed_back, cosine, sine):
    rows, width = heads_all.shape
    heads = width // 3 // HD

    def spec(part):
        return pl.BlockSpec((SEQ, HD), lambda s, h, *_: (s, part * heads + h))

    table = pl.BlockSpec((SEQ, HD), lambda s, h, *_: (0, 0))
    return pl.pallas_call(
        functools.partial(attend_back_kernel, heads),
        grid_spec=pltpu.PrefetchScalarGridSpec(
            num_scalar_prefetch=1,
            grid=(rows // SEQ, heads),
            in_specs=[spec(0), spec(1), spec(2), spec(0), table, table],
            out_specs=pl.BlockSpec((SEQ, width), lambda s, h, *_: (s, 0)),
            scratch_shapes=[pltpu.VMEM((SEQ, HD), jnp.float32), pltpu.VMEM((SEQ, HD), jnp.float32)],
        ),
        out_shape=jax.ShapeDtypeStruct((rows, width), jnp.bfloat16),
        compiler_params=pltpu.CompilerParams(vmem_limit_bytes=VMEM),
        cost_estimate=pl.CostEstimate(flops=1, bytes_accessed=1, transcendentals=0),
    )(lengths, heads_all, heads_all, heads_all, mixed_back, cosine, sine)


def feed_kernel(
    count,
    places_ref,
    normed_ref,
    back_ref,
    down_ref,
    *rest,
):
    pieces = rest[:count]
    hidden_ref, pair_back_ref, total_ref, total, pair, arrived = rest[count:]
    rows = normed_ref.shape[0]
    cols = down_ref.shape[0]
    depth = pieces[0].shape[1]
    now = pl.program_id(0)
    first = now == 0
    last = now == pl.num_programs(0) - 1

    def copies(step, slot):
        columns = pl.ds(pl.multiple_of(step * cols, cols), cols)
        return [
            pltpu.make_async_copy(
                piece.at[:, :, columns],
                pair.at[slot, :, pl.ds(pl.multiple_of(places_ref[n] * depth, depth), depth), :],
                arrived.at[slot, n],
            )
            for n, piece in enumerate(pieces)
        ]

    @pl.when(first)
    def _():
        for copy in copies(0, 0):
            copy.start()

    slot = lax.rem(now, 2)
    for copy in copies(now, slot):
        copy.wait()

    @pl.when(now < pl.num_programs(0) - 1)
    def _():
        for copy in copies(now + 1, 1 - slot):
            copy.start()

    step = min(1024, rows)
    for begin in range(0, rows, step):
        span = slice(begin, begin + step)
        normed = normed_ref[span]
        gate = jnp.dot(normed, pair[slot, 0], preferred_element_type=jnp.float32)
        up = jnp.dot(normed, pair[slot, 1], preferred_element_type=jnp.float32)
        hidden_back = transposed_dot(back_ref[span], down_ref[...])
        gate_sig = 1.0 / (1.0 + jnp.exp(-gate))
        silu = gate * gate_sig
        hidden_ref[span] = (silu * up).astype(hidden_ref.dtype)
        gate_back = (hidden_back * up * (gate_sig * (1.0 + gate * (1.0 - gate_sig)))).astype(
            jnp.bfloat16
        )
        up_back = (hidden_back * silu).astype(jnp.bfloat16)
        pair_back_ref[0, span] = gate_back
        pair_back_ref[1, span] = up_back
        part = transposed_dot(gate_back, pair[slot, 0]) + transposed_dot(up_back, pair[slot, 1])
        part = jnp.where(first, part, total[span] + part)
        total[span] = part

        @pl.when(last)
        def _(part=part, span=span):
            total_ref[span] = part.astype(total_ref.dtype)


def feed_forward(normed_two, cotangent, pieces, places, down_weight):
    rows, width = normed_two.shape
    hidden = down_weight.shape[0]
    cols = min(512, hidden)
    whole = pl.BlockSpec((rows, width), lambda j, *_: (0, 0), pipeline_mode=pl.Buffered(1))
    return pl.pallas_call(
        functools.partial(feed_kernel, len(pieces)),
        grid_spec=pltpu.PrefetchScalarGridSpec(
            num_scalar_prefetch=1,
            grid=(hidden // cols,),
            in_specs=[whole, whole, pl.BlockSpec((cols, width), lambda j, *_: (j, 0))]
            + [pl.BlockSpec(memory_space=pl.ANY)] * len(pieces),
            out_specs=[
                pl.BlockSpec((rows, cols), lambda j, *_: (0, j)),
                pl.BlockSpec((2, rows, cols), lambda j, *_: (0, 0, j)),
                pl.BlockSpec((rows, width), lambda j, *_: (0, 0), pipeline_mode=pl.Buffered(1)),
            ],
            scratch_shapes=[
                pltpu.VMEM((rows, width), jnp.float32),
                pltpu.VMEM((2, 2, width, cols), jnp.bfloat16),
                pltpu.SemaphoreType.DMA((2, len(pieces))),
            ],
        ),
        out_shape=[
            jax.ShapeDtypeStruct((rows, hidden), jnp.bfloat16),
            jax.ShapeDtypeStruct((2, rows, hidden), jnp.bfloat16),
            jax.ShapeDtypeStruct((rows, width), jnp.bfloat16),
        ],
        compiler_params=pltpu.CompilerParams(vmem_limit_bytes=VMEM),
        cost_estimate=pl.CostEstimate(flops=1, bytes_accessed=1, transcendentals=0),
    )(jnp.stack(places).astype(jnp.int32), normed_two, cotangent, down_weight, *pieces)


def middle_kernel(count, owners_ref, tokens_ref, gain_ref, out_ref, *rest):
    middle_ref, normed_ref = rest[count:]
    depth = rest[0].shape[1]
    middle = tokens_ref[...].astype(jnp.float32)
    for n, part_ref in enumerate(rest[:count]):
        rows_of = pl.ds(pl.multiple_of(owners_ref[n] * depth, depth), depth)
        middle += jnp.dot(part_ref[...], out_ref[rows_of, :], preferred_element_type=jnp.float32)
    middle_ref[...] = middle
    inverse = lax.rsqrt(jnp.mean(middle * middle, axis=-1, keepdims=True) + norm_eps)
    normed_ref[...] = (middle * inverse * gain_ref[...]).astype(normed_ref.dtype)


def finish_middle(parts, owners, out_weight, tokens, gain):
    rows, width = tokens.shape
    depth = parts[0].shape[1]
    count = len(parts)
    step = min(512, rows)

    def by_rows(cols):
        return pl.BlockSpec((step, cols), lambda i, *_: (i, 0))

    return pl.pallas_call(
        functools.partial(middle_kernel, count),
        grid_spec=pltpu.PrefetchScalarGridSpec(
            num_scalar_prefetch=1,
            grid=(rows // step,),
            in_specs=[
                by_rows(width),
                pl.BlockSpec((1, width), lambda i, *_: (0, 0)),
                pl.BlockSpec(out_weight.shape, lambda i, *_: (0, 0), pipeline_mode=pl.Buffered(1)),
            ]
            + [by_rows(depth)] * count,
            out_specs=[by_rows(width), by_rows(width)],
        ),
        out_shape=[
            jax.ShapeDtypeStruct((rows, width), jnp.float32),
            jax.ShapeDtypeStruct((rows, width), jnp.bfloat16),
        ],
        compiler_params=pltpu.CompilerParams(vmem_limit_bytes=VMEM),
        cost_estimate=pl.CostEstimate(flops=1, bytes_accessed=1, transcendentals=0),
    )(jnp.stack(owners).astype(jnp.int32), tokens, gain, out_weight, *parts)


def tie(value, *others):
    def kernel(*refs):
        pass

    return pl.pallas_call(
        kernel,
        in_specs=[pl.BlockSpec(memory_space=pl.ANY)] * (1 + len(others)),
        out_specs=pl.BlockSpec(memory_space=pl.ANY),
        out_shape=jax.ShapeDtypeStruct(value.shape, value.dtype),
        input_output_aliases={0: 0},
    )(value, *others)


def local(
    tokens,
    cotangent,
    lengths,
    qkv_weight,
    out_weight,
    gate_up_weight,
    down_weight,
    norm_gains,
    qkv_first,
    out_first,
    gate_up_first,
    down_first,
    gains_first,
    qkv_second,
    out_second,
    gate_up_second,
    down_second,
    gains_second,
):
    bf16 = jnp.bfloat16
    f32 = jnp.float32
    size = lax.axis_size("mp")
    me = lax.axis_index("mp")
    head_cols = qkv_weight.shape[2]
    row_count = tokens.shape[0] // size
    row_start = me * row_count

    def own_rows(block):
        return lax.dynamic_slice_in_dim(block, row_start, row_count, 0)

    def gather(shard, axis):
        return lax.all_gather(shard, "dp", axis=axis, tiled=True)

    qkv_low = qkv_weight.astype(bf16).reshape(qkv_weight.shape[0], -1)
    qkv_full = gather(qkv_low, 0)
    gain_low = gather(norm_gains.astype(bf16), 1)
    out_low = out_weight.astype(bf16)
    out_parts = shift_all(lambda k: out_low)
    out_rows = jnp.zeros((size,) + out_weight.shape, bf16)
    for k in range(size):
        out_rows = lax.dynamic_update_index_in_dim(
            out_rows, out_parts[k], lax.rem(me - k + size, size), 0
        )
    out_full = gather(out_rows.reshape(-1, out_weight.shape[1]), 1)
    pair_low = tie(gate_up_weight.astype(bf16).transpose(1, 0, 2), qkv_full)
    near, halves = gather_near(pair_low)
    down_full = gather(down_weight.astype(bf16), 1)

    cosine, sine_table = rope_tables()
    cosine_wide = jnp.concatenate([cosine, cosine], axis=1)
    sine_wide = jnp.concatenate([-sine_table, sine_table], axis=1)
    gain_one = gain_low[0].astype(f32)
    gain_two = gain_low[1].astype(f32)
    normed, scale_one = norm_forward(tokens.astype(f32), gain_one)
    normed_bf = lax.optimization_barrier(normed.astype(bf16))
    heads_all = project_heads(normed_bf, qkv_full, cosine_wide, sine_wide)
    mixed_bf = attend(lengths, heads_all)
    parts, owners = gather_line(mixed_bf)
    mixed_own = jnp.zeros((row_count, size, head_cols), bf16)
    for part, owner in zip(parts[1:] + parts[:1], owners[1:] + owners[:1]):
        mixed_own = lax.dynamic_update_slice_in_dim(mixed_own, own_rows(part)[:, None], owner, 1)
    mixed_own = mixed_own.reshape(row_count, size * head_cols)
    middle, normed_two = finish_middle(parts, owners, out_full, tokens, gain_two[None])

    pieces, places = gather_far(near, halves, normed_two)
    hidden, pair_back, two_back_part = feed_forward(
        normed_two, cotangent, pieces, places, down_full
    )
    two_back = lax.psum_scatter(two_back_part, "mp", scatter_dimension=0, tiled=True)
    feed_part = jnp.dot(hidden, down_full, preferred_element_type=f32).astype(bf16)
    pair_red, pair_total = reduce_dp(
        lambda columns: [lead_dot(columns, pair_back[k]) for k in range(2)], normed_two, 0
    )
    half = hidden.shape[1] // 2
    down_red, down_total = reduce_dp(
        lambda columns: [lead_dot(hidden[:, k * half : (k + 1) * half], columns) for k in range(2)],
        cotangent,
        1,
    )
    two_back = two_back.astype(f32)

    middle_own = own_rows(middle)
    _, scale_two = norm_forward(middle_own, gain_two)
    middle_back, gain_two_grad = norm_backward(middle_own, scale_two, gain_two, two_back)
    middle_back = middle_back + own_rows(cotangent).astype(f32)
    middle_low = middle_back.astype(bf16)
    mixed_back = jnp.einsum("nd,ad->na", middle_low, out_full, preferred_element_type=f32).astype(
        bf16
    )
    back_parts = shift_all(lambda k: pick(mixed_back, lax.rem(me + k, size), head_cols, 1))
    mixed_heads = jnp.zeros((size, row_count, head_cols), bf16)
    for k in range(size):
        mixed_heads = lax.dynamic_update_index_in_dim(
            mixed_heads, back_parts[k], lax.rem(me - k + size, size), 0
        )
    feed_part = tie(feed_part, *back_parts)
    feed_out = lax.psum_scatter(feed_part, "mp", scatter_dimension=0, tiled=True)
    half = mixed_own.shape[1] // 2
    out_red, out_total = reduce_dp(
        lambda columns: [
            lead_dot(mixed_own[:, k * half : (k + 1) * half], columns) for k in range(2)
        ],
        middle_low,
        1,
    )
    out_red = jnp.concatenate(out_red, axis=0).astype(bf16)
    out_sum = shift_all(lambda k: pick(out_red, lax.rem(me + k, size), head_cols, 0))
    out_sum = sum(part.astype(f32) for part in out_sum)
    mixed_heads = tie(mixed_heads.reshape(-1, head_cols), *out_total)

    project_back = attend_back(
        lengths, heads_all, mixed_heads, cosine_wide, -sine_wide
    )
    one_back_part = transposed_dot(project_back, qkv_full).astype(bf16)
    one_back = lax.psum_scatter(tie(one_back_part, feed_out), "mp", scatter_dimension=0, tiled=True).astype(f32)
    gain_one_grad = jnp.sum(one_back_part.astype(f32) * tokens.astype(f32) * scale_one, axis=0)
    half = project_back.shape[1] // 2
    qkv_red, _ = reduce_dp(
        lambda columns: [
            lead_dot(columns, project_back[:, k * half : (k + 1) * half]) for k in range(2)
        ],
        tie(normed_bf, one_back_part),
        0,
    )
    qkv_red = jnp.concatenate(qkv_red, axis=1)
    qkv_grad = tie(
        jnp.stack([qkv_red[:, c * head_cols : (c + 1) * head_cols] for c in range(3)])
    ).transpose(1, 0, 2)
    gains_sum = sum_flips(jnp.stack([gain_one_grad, gain_two_grad]), "dp")
    gains_sum = pick(gains_sum, lax.axis_index("dp"), norm_gains.shape[1], 1)
    gains_red = sum_flips(gains_sum, "mp")

    tokens_part, _ = norm_backward(
        own_rows(tokens).astype(f32), own_rows(scale_one), gain_one, one_back
    )
    tokens_grad = tokens_part + middle_back
    block_out = (middle_own + feed_out.astype(f32)).astype(bf16)
    rates = step_rates()
    pair_grad = tie(jnp.stack(pair_red, axis=1))
    qkv_all = adamw(qkv_weight, qkv_first, qkv_second, qkv_grad, rates[0])
    out_all = adamw(out_weight, out_first, out_second, out_sum, rates[1])
    gate_up_all = adamw(gate_up_weight, gate_up_first, gate_up_second, pair_grad, rates[2])
    down_all = adamw(down_weight, down_first, down_second, jnp.concatenate(down_red, axis=0), rates[3])
    gains_all = adamw(norm_gains, gains_first, gains_second, gains_red, rates[4])
    states = (qkv_all, out_all, gate_up_all, down_all, gains_all)
    return (block_out, tokens_grad) + tuple(state[j] for j in range(3) for state in states)


def solution(mesh):
    in_specs = (
        P("dp", None),
        P("dp", None),
        P("dp"),
        P("dp", None, "mp"),
        P("mp", "dp"),
        P("dp", None, "mp"),
        P("mp", "dp"),
        P(None, "dp"),
        P("dp", None, "mp"),
        P("mp", "dp"),
        P("dp", None, "mp"),
        P("mp", "dp"),
        P(None, "dp"),
        P("dp", None, "mp"),
        P("mp", "dp"),
        P("dp", None, "mp"),
        P("mp", "dp"),
        P(None, "dp"),
    )
    out_specs = (
        P(("dp", "mp"), None),
        P(("dp", "mp"), None),
        P("dp", None, "mp"),
        P("mp", "dp"),
        P("dp", None, "mp"),
        P("mp", "dp"),
        P(None, "dp"),
        P("dp", None, "mp"),
        P("mp", "dp"),
        P("dp", None, "mp"),
        P("mp", "dp"),
        P(None, "dp"),
        P("dp", None, "mp"),
        P("mp", "dp"),
        P("dp", None, "mp"),
        P("mp", "dp"),
        P(None, "dp"),
    )
    return jax.shard_map(local, mesh=mesh, in_specs=in_specs, out_specs=out_specs, check_vma=False)
```

```python
import functools
import math

import jax
import jax.numpy as jnp
from jax import lax
from jax.experimental import pallas as pl
from jax.experimental.pallas import tpu as pltpu
from jax.sharding import PartitionSpec as P

D = 2048
H = 16
HD = 128
FF = 8192
SEQ = 1024
STEP = 10
VMEM = 56 << 20


norm_eps = 1e-05
adam_eps = 1e-08
beta_first = 0.5
beta_second = 0.5
weight_decay = 0.1


def step_rates():
    return (
        0.8 / math.sqrt(D),
        0.8 / math.sqrt(max(1, 2 * H * HD // SEQ)),
        0.8 / math.sqrt(D),
        0.8 / math.sqrt(FF),
        0.4,
    )


def rope_tables():
    halfway = HD // 2
    inverse = jnp.exp(-math.log(10000.0) * jnp.arange(halfway, dtype=jnp.float32) * 2.0 / HD)
    angles = jnp.arange(SEQ, dtype=jnp.float32)[:, None] * inverse[None, :]
    return (jnp.cos(angles), jnp.sin(angles))


def norm_forward(values, gain):
    inverse = lax.rsqrt(jnp.mean(values * values, axis=-1, keepdims=True) + norm_eps)
    return (values * inverse * gain, inverse)


def norm_backward(values, inverse, gain, upstream):
    scaled = upstream * gain
    gain_grad = jnp.sum(upstream * values * inverse, axis=0)
    values_grad = inverse * scaled - values * inverse * inverse * inverse * jnp.mean(
        scaled * values, axis=-1, keepdims=True
    )
    return (values_grad, gain_grad)


def adamw(weight, moment_one, moment_two, gradient, step_rate):
    first_new = beta_first * moment_one + (1.0 - beta_first) * gradient
    second_new = beta_second * moment_two + (1.0 - beta_second) * gradient * gradient
    first_hat = first_new / (1.0 - beta_first**STEP)
    second_hat = second_new / (1.0 - beta_second**STEP)
    weight_new = weight - step_rate * (
        first_hat / (jnp.sqrt(second_hat) + adam_eps) + weight_decay * weight
    )
    return (weight_new, first_new, second_new)


CORE, ALONG_X, ALONG_Y = 1, 2, 4
DIAGONAL = ALONG_X + ALONG_Y


def flip(block, bits, name="dp"):
    return lax.ppermute(block, name, [(j, j ^ bits) for j in range(lax.axis_size(name))])


def pick(block, place, width, axis):
    return lax.dynamic_slice_in_dim(block, place * width, width, axis)


def gather_near(shard):
    if lax.axis_size("dp") != 8:
        return [lax.all_gather(shard, "dp", axis=1, tiled=True)], None
    from_x = flip(shard, ALONG_X)
    from_y = flip(shard, ALONG_Y)
    from_core = flip(shard, CORE)
    upper = flip(from_y[:1], ALONG_X)
    lower = flip(from_x[1:], ALONG_Y)
    near = [shard, from_core, from_x, from_y, flip(from_x, CORE), flip(from_y, CORE)]
    return near, (upper, lower)


def gather_far(near, halves, after):
    if halves is None:
        return near, [0]
    me = lax.axis_index("dp")
    upper, lower = halves
    far = jnp.concatenate([tie(upper, after), tie(lower, after)], axis=0)
    bits = [0, CORE, ALONG_X, ALONG_Y, ALONG_X + CORE, ALONG_Y + CORE, DIAGONAL, DIAGONAL + CORE]
    return near + [far, flip(far, CORE)], [me ^ b for b in bits]


def core_columns(block, core):
    width = block.shape[1] // 8
    return jnp.concatenate([pick(block, 2 * q + core, width, 1) for q in range(4)], axis=1)


def reduce_dp(products, sharded, axis, after=()):
    f32, bf16 = jnp.float32, jnp.bfloat16
    if lax.axis_size("dp") != 8:
        full = [part.astype(bf16) for part in products(sharded)]
        done = [lax.psum_scatter(part, "dp", scatter_dimension=axis, tiled=True) for part in full]
        return [part.astype(f32) for part in done], full
    me = lax.axis_index("dp")
    core = lax.rem(me, 2)
    chip = lax.div(me, 2)
    other = [part.astype(bf16) for part in products(core_columns(sharded, 1 - core))]
    other = [flip(part, CORE) for part in other]
    own = products(core_columns(sharded, core))
    total = [(a + b.astype(f32)).astype(bf16) for a, b in zip(own, other)]
    width = total[0].shape[axis] // 4
    upper = flip(pick(total[0], chip ^ 3, width, axis), ALONG_X)
    lower = flip(pick(total[1], chip ^ 3, width, axis), ALONG_Y)
    if after:
        upper, lower = tie(upper, *after), tie(lower, *after)
    near_x = [pick(part, chip ^ 1, width, axis) for part in total]
    near_y = [pick(part, chip ^ 2, width, axis) for part in total]
    to_x = jnp.stack([near_x[0], (near_x[1].astype(f32) + lower.astype(f32)).astype(bf16)])
    to_y = jnp.stack([(near_y[0].astype(f32) + upper.astype(f32)).astype(bf16), near_y[1]])
    from_x = flip(to_x, ALONG_X)
    from_y = flip(to_y, ALONG_Y)
    mine = [pick(part, chip, width, axis).astype(f32) for part in total]
    return [mine[k] + from_x[k].astype(f32) + from_y[k].astype(f32) for k in range(2)], total


def shift_all(take):
    size = lax.axis_size("mp")
    got = [take(0)]
    for k in range(1, size):
        got.append(lax.ppermute(take(k), "mp", [(j, (j + k) % size) for j in range(size)]))
    return got


def gather_line(block):
    size = lax.axis_size("mp")
    me = lax.axis_index("mp")
    if size != 4:
        parts = shift_all(lambda k: block)
        return parts, [lax.rem(me - k + size, size) for k in range(size)]
    from_low = lax.ppermute(block, "mp", [(0, 1), (1, 2), (2, 3)])
    from_high = lax.ppermute(block, "mp", [(1, 0), (2, 1), (3, 2)])
    inward = jnp.where(me == 1, from_low, from_high)
    outward = jnp.where(me == 1, from_high, from_low)
    end = lax.ppermute(inward, "mp", [(2, 0), (1, 3)])
    middle = lax.ppermute(inward, "mp", [(2, 1), (1, 2)])
    edge = lax.ppermute(outward, "mp", [(1, 0), (2, 3)])
    low, high = lax.rem(me + 3, 4), lax.rem(me + 1, 4)
    end_owner = jnp.where(me == 0, 3, jnp.where(me == 3, 0, me))
    return [block, from_low, from_high, end, middle + edge], [
        me,
        low,
        high,
        end_owner,
        lax.rem(me + 2, 4),
    ]


def sum_flips(block, name):
    bits = 1
    while bits < lax.axis_size(name):
        block = block + flip(block, bits, name)
        bits *= 2
    return block


def rotate_wide(block, cosine, sine):
    heads = block.shape[1] // HD
    parts = []
    for h in range(heads):
        head = block[:, h * HD : (h + 1) * HD]
        parts.append(head * cosine + pltpu.roll(head, HD // 2, 1) * sine)
    return parts[0] if heads == 1 else jnp.concatenate(parts, axis=1)


def project_kernel(normed_ref, weight_ref, cosine_ref, sine_ref, out_ref):
    rows = normed_ref.shape[0]
    step = min(1024, rows)
    for begin in range(0, rows, step):
        block = jnp.dot(
            normed_ref[begin : begin + step], weight_ref[...], preferred_element_type=jnp.float32
        )

        @pl.when(pl.program_id(0) < 2)
        def _(block=block, begin=begin):
            out_ref[begin : begin + step] = rotate_wide(
                block, cosine_ref[begin : begin + step], sine_ref[begin : begin + step]
            ).astype(out_ref.dtype)

        @pl.when(pl.program_id(0) == 2)
        def _(block=block, begin=begin):
            out_ref[begin : begin + step] = block.astype(out_ref.dtype)


def project_heads(normed, weight, cosine, sine):
    rows, width = normed.shape
    cols = weight.shape[1] // 3
    return pl.pallas_call(
        project_kernel,
        grid=(3,),
        in_specs=[
            pl.BlockSpec((rows, width), lambda c: (0, 0)),
            pl.BlockSpec((width, cols), lambda c: (0, c)),
            pl.BlockSpec((rows, HD), lambda c: (0, 0)),
            pl.BlockSpec((rows, HD), lambda c: (0, 0)),
        ],
        out_specs=pl.BlockSpec((rows, cols), lambda c: (0, c)),
        out_shape=jax.ShapeDtypeStruct((rows, 3 * cols), jnp.bfloat16),
        compiler_params=pltpu.CompilerParams(vmem_limit_bytes=VMEM),
        cost_estimate=pl.CostEstimate(flops=1, bytes_accessed=1, transcendentals=0),
    )(normed, weight, cosine, sine)


def transposed_dot(a, b):
    return lax.dot_general(a, b, (((1,), (1,)), ((), ())), preferred_element_type=jnp.float32)


def lead_dot(a, b):
    return lax.dot_general(a, b, (((0,), (0,)), ((), ())), preferred_element_type=jnp.float32)


def causal_sigmoid(scores_raw, begin):
    rows, cols = scores_raw.shape
    grown = jnp.exp(math.log(SEQ) - scores_raw * (1.0 / math.sqrt(HD)))
    sigmoid_val = 1.0 / (1.0 + grown)
    row_ids = begin + lax.broadcasted_iota(jnp.int32, (rows, rows), 0)
    col_ids = begin + lax.broadcasted_iota(jnp.int32, (rows, rows), 1)
    last = jnp.where(col_ids <= row_ids, sigmoid_val[:, cols - rows :], 0.0)
    if cols == rows:
        return last
    return jnp.concatenate([sigmoid_val[:, : cols - rows], last], axis=1)


def keep_valid(block, valid_len):
    ids = lax.broadcasted_iota(jnp.int32, block.shape, 0)
    return jnp.where(ids < valid_len, block, jnp.zeros_like(block))


def attend_kernel(lengths_ref, query_ref, key_ref, value_ref, out_ref):
    valid_len = lengths_ref[pl.program_id(0)]
    keys = key_ref[...]
    values = keep_valid(value_ref[...], valid_len)
    step = min(256, SEQ)
    for begin in range(0, SEQ, step):
        end = begin + step
        weights = causal_sigmoid(transposed_dot(query_ref[begin:end], keys[:end]), begin)
        out_ref[begin:end] = jnp.dot(
            weights.astype(jnp.bfloat16), values[:end], preferred_element_type=jnp.float32
        ).astype(out_ref.dtype)


def attend(lengths, heads_all):
    rows, width = heads_all.shape
    heads = width // 3 // HD

    def spec(part):
        return pl.BlockSpec((SEQ, HD), lambda s, h, *_: (s, part * heads + h))

    return pl.pallas_call(
        attend_kernel,
        grid_spec=pltpu.PrefetchScalarGridSpec(
            num_scalar_prefetch=1,
            grid=(rows // SEQ, heads),
            in_specs=[spec(0), spec(1), spec(2)],
            out_specs=pl.BlockSpec((SEQ, HD), lambda s, h, *_: (s, h)),
        ),
        out_shape=jax.ShapeDtypeStruct((rows, width // 3), jnp.bfloat16),
        compiler_params=pltpu.CompilerParams(vmem_limit_bytes=VMEM),
        cost_estimate=pl.CostEstimate(flops=1, bytes_accessed=1, transcendentals=0),
    )(lengths, heads_all, heads_all, heads_all)


def attend_back_kernel(
    heads,
    lengths_ref,
    query_ref,
    key_ref,
    value_ref,
    back_ref,
    cosine_ref,
    sine_ref,
    out_ref,
    key_total,
    value_total,
):
    valid_len = lengths_ref[pl.program_id(0)]
    head = pl.program_id(1)
    keys = key_ref[...]
    keys_kept = keep_valid(keys, valid_len)
    values = value_ref[...]
    key_total[...] = jnp.zeros_like(key_total)
    value_total[...] = jnp.zeros_like(value_total)
    step = min(256, SEQ)

    def column(part):
        return pl.ds(pl.multiple_of(part * heads * HD + head * HD, HD), HD)

    for begin in range(0, SEQ, step):
        end = begin + step
        queries = query_ref[begin:end]
        back = back_ref[begin:end]
        weights = causal_sigmoid(transposed_dot(queries, keys[:end]), begin)
        value_total[:end] += lead_dot(weights.astype(jnp.bfloat16), back)
        weight_back = transposed_dot(back, values[:end])
        score_back = (weight_back * (weights * (1.0 - weights))).astype(jnp.bfloat16)
        query_back = jnp.dot(
            score_back, keys_kept[:end], preferred_element_type=jnp.float32
        ) * (1.0 / math.sqrt(HD))
        key_total[:end] += lead_dot(score_back, queries)
        out_ref[begin:end, column(0)] = rotate_wide(
            query_back, cosine_ref[begin:end], sine_ref[begin:end]
        ).astype(out_ref.dtype)
    key_back = keep_valid(key_total[...] * (1.0 / math.sqrt(HD)), valid_len)
    out_ref[:, column(1)] = rotate_wide(key_back, cosine_ref[...], sine_ref[...]).astype(
        out_ref.dtype
    )
    out_ref[:, column(2)] = keep_valid(value_total[...], valid_len).astype(out_ref.dtype)


def attend_back(lengths, heads_all, mixed_back, cosine, sine):
    rows, width = heads_all.shape
    heads = width // 3 // HD

    def spec(part):
        return pl.BlockSpec((SEQ, HD), lambda s, h, *_: (s, part * heads + h))

    table = pl.BlockSpec((SEQ, HD), lambda s, h, *_: (0, 0))
    return pl.pallas_call(
        functools.partial(attend_back_kernel, heads),
        grid_spec=pltpu.PrefetchScalarGridSpec(
            num_scalar_prefetch=1,
            grid=(rows // SEQ, heads),
            in_specs=[spec(0), spec(1), spec(2), spec(0), table, table],
            out_specs=pl.BlockSpec((SEQ, width), lambda s, h, *_: (s, 0)),
            scratch_shapes=[pltpu.VMEM((SEQ, HD), jnp.float32), pltpu.VMEM((SEQ, HD), jnp.float32)],
        ),
        out_shape=jax.ShapeDtypeStruct((rows, width), jnp.bfloat16),
        compiler_params=pltpu.CompilerParams(vmem_limit_bytes=VMEM),
        cost_estimate=pl.CostEstimate(flops=1, bytes_accessed=1, transcendentals=0),
    )(lengths, heads_all, heads_all, heads_all, mixed_back, cosine, sine)


def feed_kernel(
    count,
    places_ref,
    normed_ref,
    back_ref,
    down_ref,
    *rest,
):
    pieces = rest[:count]
    hidden_ref, pair_back_ref, total_ref, total, pair, arrived = rest[count:]
    rows = normed_ref.shape[0]
    cols = down_ref.shape[0]
    depth = pieces[0].shape[1]
    now = pl.program_id(0)
    first = now == 0
    last = now == pl.num_programs(0) - 1

    def copies(step, slot):
        columns = pl.ds(pl.multiple_of(step * cols, cols), cols)
        return [
            pltpu.make_async_copy(
                piece.at[:, :, columns],
                pair.at[slot, :, pl.ds(pl.multiple_of(places_ref[n] * depth, depth), depth), :],
                arrived.at[slot, n],
            )
            for n, piece in enumerate(pieces)
        ]

    @pl.when(first)
    def _():
        for copy in copies(0, 0):
            copy.start()

    slot = lax.rem(now, 2)
    for copy in copies(now, slot):
        copy.wait()

    @pl.when(now < pl.num_programs(0) - 1)
    def _():
        for copy in copies(now + 1, 1 - slot):
            copy.start()

    step = min(1024, rows)
    for begin in range(0, rows, step):
        span = slice(begin, begin + step)
        normed = normed_ref[span]
        gate = jnp.dot(normed, pair[slot, 0], preferred_element_type=jnp.float32)
        up = jnp.dot(normed, pair[slot, 1], preferred_element_type=jnp.float32)
        hidden_back = transposed_dot(back_ref[span], down_ref[...])
        gate_sig = 1.0 / (1.0 + jnp.exp(-gate))
        silu = gate * gate_sig
        hidden_ref[span] = (silu * up).astype(hidden_ref.dtype)
        gate_back = (hidden_back * up * (gate_sig * (1.0 + gate * (1.0 - gate_sig)))).astype(
            jnp.bfloat16
        )
        up_back = (hidden_back * silu).astype(jnp.bfloat16)
        pair_back_ref[0, span] = gate_back
        pair_back_ref[1, span] = up_back
        part = transposed_dot(gate_back, pair[slot, 0]) + transposed_dot(up_back, pair[slot, 1])
        part = jnp.where(first, part, total[span] + part)
        total[span] = part

        @pl.when(last)
        def _(part=part, span=span):
            total_ref[span] = part.astype(total_ref.dtype)


def feed_forward(normed_two, cotangent, pieces, places, down_weight):
    rows, width = normed_two.shape
    hidden = down_weight.shape[0]
    cols = min(512, hidden)
    whole = pl.BlockSpec((rows, width), lambda j, *_: (0, 0), pipeline_mode=pl.Buffered(1))
    return pl.pallas_call(
        functools.partial(feed_kernel, len(pieces)),
        grid_spec=pltpu.PrefetchScalarGridSpec(
            num_scalar_prefetch=1,
            grid=(hidden // cols,),
            in_specs=[whole, whole, pl.BlockSpec((cols, width), lambda j, *_: (j, 0))]
            + [pl.BlockSpec(memory_space=pl.ANY)] * len(pieces),
            out_specs=[
                pl.BlockSpec((rows, cols), lambda j, *_: (0, j)),
                pl.BlockSpec((2, rows, cols), lambda j, *_: (0, 0, j)),
                pl.BlockSpec((rows, width), lambda j, *_: (0, 0), pipeline_mode=pl.Buffered(1)),
            ],
            scratch_shapes=[
                pltpu.VMEM((rows, width), jnp.float32),
                pltpu.VMEM((2, 2, width, cols), jnp.bfloat16),
                pltpu.SemaphoreType.DMA((2, len(pieces))),
            ],
        ),
        out_shape=[
            jax.ShapeDtypeStruct((rows, hidden), jnp.bfloat16),
            jax.ShapeDtypeStruct((2, rows, hidden), jnp.bfloat16),
            jax.ShapeDtypeStruct((rows, width), jnp.bfloat16),
        ],
        compiler_params=pltpu.CompilerParams(vmem_limit_bytes=VMEM),
        cost_estimate=pl.CostEstimate(flops=1, bytes_accessed=1, transcendentals=0),
    )(jnp.stack(places).astype(jnp.int32), normed_two, cotangent, down_weight, *pieces)


def middle_kernel(count, owners_ref, tokens_ref, gain_ref, out_ref, *rest):
    middle_ref, normed_ref = rest[count:]
    depth = rest[0].shape[1]
    middle = tokens_ref[...].astype(jnp.float32)
    for n, part_ref in enumerate(rest[:count]):
        rows_of = pl.ds(pl.multiple_of(owners_ref[n] * depth, depth), depth)
        middle += jnp.dot(part_ref[...], out_ref[rows_of, :], preferred_element_type=jnp.float32)
    middle_ref[...] = middle
    inverse = lax.rsqrt(jnp.mean(middle * middle, axis=-1, keepdims=True) + norm_eps)
    normed_ref[...] = (middle * inverse * gain_ref[...]).astype(normed_ref.dtype)


def finish_middle(parts, owners, out_weight, tokens, gain):
    rows, width = tokens.shape
    depth = parts[0].shape[1]
    count = len(parts)
    step = min(512, rows)

    def by_rows(cols):
        return pl.BlockSpec((step, cols), lambda i, *_: (i, 0))

    return pl.pallas_call(
        functools.partial(middle_kernel, count),
        grid_spec=pltpu.PrefetchScalarGridSpec(
            num_scalar_prefetch=1,
            grid=(rows // step,),
            in_specs=[
                by_rows(width),
                pl.BlockSpec((1, width), lambda i, *_: (0, 0)),
                pl.BlockSpec(out_weight.shape, lambda i, *_: (0, 0), pipeline_mode=pl.Buffered(1)),
            ]
            + [by_rows(depth)] * count,
            out_specs=[by_rows(width), by_rows(width)],
        ),
        out_shape=[
            jax.ShapeDtypeStruct((rows, width), jnp.float32),
            jax.ShapeDtypeStruct((rows, width), jnp.bfloat16),
        ],
        compiler_params=pltpu.CompilerParams(vmem_limit_bytes=VMEM),
        cost_estimate=pl.CostEstimate(flops=1, bytes_accessed=1, transcendentals=0),
    )(jnp.stack(owners).astype(jnp.int32), tokens, gain, out_weight, *parts)


def tie(value, *others):
    def kernel(*refs):
        pass

    return pl.pallas_call(
        kernel,
        in_specs=[pl.BlockSpec(memory_space=pl.ANY)] * (1 + len(others)),
        out_specs=pl.BlockSpec(memory_space=pl.ANY),
        out_shape=jax.ShapeDtypeStruct(value.shape, value.dtype),
        input_output_aliases={0: 0},
    )(value, *others)


def local(
    tokens,
    cotangent,
    lengths,
    qkv_weight,
    out_weight,
    gate_up_weight,
    down_weight,
    norm_gains,
    qkv_first,
    out_first,
    gate_up_first,
    down_first,
    gains_first,
    qkv_second,
    out_second,
    gate_up_second,
    down_second,
    gains_second,
):
    bf16 = jnp.bfloat16
    f32 = jnp.float32
    size = lax.axis_size("mp")
    me = lax.axis_index("mp")
    head_cols = qkv_weight.shape[2]
    row_count = tokens.shape[0] // size
    row_start = me * row_count

    def own_rows(block):
        return lax.dynamic_slice_in_dim(block, row_start, row_count, 0)

    def gather(shard, axis):
        return lax.all_gather(shard, "dp", axis=axis, tiled=True)

    qkv_low = qkv_weight.astype(bf16).reshape(qkv_weight.shape[0], -1)
    qkv_full = gather(qkv_low, 0)
    gain_low = gather(norm_gains.astype(bf16), 1)
    out_low = out_weight.astype(bf16)
    out_parts = shift_all(lambda k: out_low)
    out_rows = jnp.zeros((size,) + out_weight.shape, bf16)
    for k in range(size):
        out_rows = lax.dynamic_update_index_in_dim(
            out_rows, out_parts[k], lax.rem(me - k + size, size), 0
        )
    out_full = gather(out_rows.reshape(-1, out_weight.shape[1]), 1)
    pair_low = tie(gate_up_weight.astype(bf16).transpose(1, 0, 2), qkv_full)
    near, halves = gather_near(pair_low)
    down_full = gather(down_weight.astype(bf16), 1)

    cosine, sine_table = rope_tables()
    cosine_wide = jnp.concatenate([cosine, cosine], axis=1)
    sine_wide = jnp.concatenate([-sine_table, sine_table], axis=1)
    gain_one = gain_low[0].astype(f32)
    gain_two = gain_low[1].astype(f32)
    normed, scale_one = norm_forward(tokens.astype(f32), gain_one)
    normed_bf = lax.optimization_barrier(normed.astype(bf16))
    heads_all = project_heads(normed_bf, qkv_full, cosine_wide, sine_wide)
    mixed_bf = attend(lengths, heads_all)
    parts, owners = gather_line(mixed_bf)
    mixed_own = jnp.zeros((row_count, size, head_cols), bf16)
    for part, owner in zip(parts[1:] + parts[:1], owners[1:] + owners[:1]):
        mixed_own = lax.dynamic_update_slice_in_dim(mixed_own, own_rows(part)[:, None], owner, 1)
    mixed_own = mixed_own.reshape(row_count, size * head_cols)
    middle, normed_two = finish_middle(parts, owners, out_full, tokens, gain_two[None])

    pieces, places = gather_far(near, halves, normed_two)
    hidden, pair_back, two_back_part = feed_forward(
        normed_two, cotangent, pieces, places, down_full
    )
    two_back = lax.psum_scatter(two_back_part, "mp", scatter_dimension=0, tiled=True)
    feed_part = jnp.dot(hidden, down_full, preferred_element_type=f32).astype(bf16)
    pair_red, pair_total = reduce_dp(
        lambda columns: [lead_dot(columns, pair_back[k]) for k in range(2)], normed_two, 0
    )
    half = hidden.shape[1] // 2
    down_red, down_total = reduce_dp(
        lambda columns: [lead_dot(hidden[:, k * half : (k + 1) * half], columns) for k in range(2)],
        cotangent,
        1,
    )
    two_back = two_back.astype(f32)

    middle_own = own_rows(middle)
    _, scale_two = norm_forward(middle_own, gain_two)
    middle_back, gain_two_grad = norm_backward(middle_own, scale_two, gain_two, two_back)
    middle_back = middle_back + own_rows(cotangent).astype(f32)
    middle_low = middle_back.astype(bf16)
    mixed_back = jnp.einsum("nd,ad->na", middle_low, out_full, preferred_element_type=f32).astype(
        bf16
    )
    back_parts = shift_all(lambda k: pick(mixed_back, lax.rem(me + k, size), head_cols, 1))
    mixed_heads = jnp.zeros((size, row_count, head_cols), bf16)
    for k in range(size):
        mixed_heads = lax.dynamic_update_index_in_dim(
            mixed_heads, back_parts[k], lax.rem(me - k + size, size), 0
        )
    feed_part = tie(feed_part, *back_parts)
    feed_out = lax.psum_scatter(feed_part, "mp", scatter_dimension=0, tiled=True)
    half = mixed_own.shape[1] // 2
    out_red, out_total = reduce_dp(
        lambda columns: [
            lead_dot(mixed_own[:, k * half : (k + 1) * half], columns) for k in range(2)
        ],
        middle_low,
        1,
    )
    out_red = jnp.concatenate(out_red, axis=0).astype(bf16)
    out_sum = shift_all(lambda k: pick(out_red, lax.rem(me + k, size), head_cols, 0))
    out_sum = sum(part.astype(f32) for part in out_sum)
    mixed_heads = tie(mixed_heads.reshape(-1, head_cols), *out_total)

    project_back = attend_back(
        lengths, heads_all, mixed_heads, cosine_wide, -sine_wide
    )
    one_back_part = transposed_dot(project_back, qkv_full).astype(bf16)
    one_back = lax.psum_scatter(tie(one_back_part, feed_out), "mp", scatter_dimension=0, tiled=True).astype(f32)
    gain_one_grad = jnp.sum(one_back_part.astype(f32) * tokens.astype(f32) * scale_one, axis=0)
    half = project_back.shape[1] // 2
    qkv_red, qkv_total = reduce_dp(
        lambda columns: [
            lead_dot(columns, project_back[:, k * half : (k + 1) * half]) for k in range(2)
        ],
        tie(normed_bf, one_back_part),
        0,
    )
    qkv_red = jnp.concatenate(qkv_red, axis=1)
    qkv_grad = tie(
        jnp.stack([qkv_red[:, c * head_cols : (c + 1) * head_cols] for c in range(3)])
    ).transpose(1, 0, 2)
    gains_sum = sum_flips(tie(jnp.stack([gain_one_grad, gain_two_grad]), *qkv_total), "dp")
    gains_sum = pick(gains_sum, lax.axis_index("dp"), norm_gains.shape[1], 1)
    gains_red = sum_flips(gains_sum, "mp")

    tokens_part, _ = norm_backward(
        own_rows(tokens).astype(f32), own_rows(scale_one), gain_one, one_back
    )
    tokens_grad = tokens_part + middle_back
    block_out = (middle_own + feed_out.astype(f32)).astype(bf16)
    rates = step_rates()
    pair_grad = tie(jnp.stack(pair_red, axis=1))
    qkv_all = adamw(qkv_weight, qkv_first, qkv_second, qkv_grad, rates[0])
    out_all = adamw(out_weight, out_first, out_second, out_sum, rates[1])
    gate_up_all = adamw(gate_up_weight, gate_up_first, gate_up_second, pair_grad, rates[2])
    down_all = adamw(down_weight, down_first, down_second, jnp.concatenate(down_red, axis=0), rates[3])
    gains_all = adamw(norm_gains, gains_first, gains_second, gains_red, rates[4])
    states = (qkv_all, out_all, gate_up_all, down_all, gains_all)
    return (block_out, tokens_grad) + tuple(state[j] for j in range(3) for state in states)


def solution(mesh):
    in_specs = (
        P("dp", None),
        P("dp", None),
        P("dp"),
        P("dp", None, "mp"),
        P("mp", "dp"),
        P("dp", None, "mp"),
        P("mp", "dp"),
        P(None, "dp"),
        P("dp", None, "mp"),
        P("mp", "dp"),
        P("dp", None, "mp"),
        P("mp", "dp"),
        P(None, "dp"),
        P("dp", None, "mp"),
        P("mp", "dp"),
        P("dp", None, "mp"),
        P("mp", "dp"),
        P(None, "dp"),
    )
    out_specs = (
        P(("dp", "mp"), None),
        P(("dp", "mp"), None),
        P("dp", None, "mp"),
        P("mp", "dp"),
        P("dp", None, "mp"),
        P("mp", "dp"),
        P(None, "dp"),
        P("dp", None, "mp"),
        P("mp", "dp"),
        P("dp", None, "mp"),
        P("mp", "dp"),
        P(None, "dp"),
        P("dp", None, "mp"),
        P("mp", "dp"),
        P("dp", None, "mp"),
        P("mp", "dp"),
        P(None, "dp"),
    )
    return jax.shard_map(local, mesh=mesh, in_specs=in_specs, out_specs=out_specs, check_vma=False)
```
